32 devices in a mesh: dp: 8 (over z, x), tensor: 4 (over y, core).
Axes of the slice: x: 2, y: 2, z: 4, core: 2. Of those that a mesh axis runs over, the one named last changes fastest.
Arguments:
- tokens_in: float32 [12544, 512], P(('dp', 'tensor')), may hold values from -6 to 6
- out_grad: float32 [12544, 512], P(('dp', 'tensor')), may hold values from -12 to 12
- w_qkv: float32 [3, 512, 512], P(None, 'dp', 'tensor'), may hold values from -0.25 to 0.25
- w_proj: float32 [512, 512], P('tensor', 'dp'), may hold values from -1 to 1
- w_fc1: float32 [512, 2048], P('dp', 'tensor'), may hold values from -0.25 to 0.25
- w_fc2: float32 [2048, 512], P('tensor', 'dp'), may hold values from -0.125 to 0.125
- small_params: float32 [12, 512], P(None, 'dp'), may hold values from -1.2 to 1.6, as said below
- bias_table: float32 [16, 169], P('tensor'), may hold values from -6 to 6
- qkv_first: float32 [3, 512, 512], P(None, 'dp', 'tensor'), may hold values from -80 to 80
- qkv_second: float32 [3, 512, 512], P(None, 'dp', 'tensor'), may hold values from 12.544 to 50.176
- proj_first: float32 [512, 512], P('tensor', 'dp'), may hold values from -32 to 32
- proj_second: float32 [512, 512], P('tensor', 'dp'), may hold values from 2.00704 to 8.02816
- fc1_first: float32 [512, 2048], P('dp', 'tensor'), may hold values from -24 to 24
- fc1_second: float32 [512, 2048], P('dp', 'tensor'), may hold values from 1.12896 to 4.51584
- fc2_first: float32 [2048, 512], P('tensor', 'dp'), may hold values from -48 to 48
- fc2_second: float32 [2048, 512], P('tensor', 'dp'), may hold values from 5.26848 to 21.3248
- small_first: float32 [12, 512], P(None, 'dp'), may hold values from -73.92 to 73.92, as said below
- small_second: float32 [12, 512], P(None, 'dp'), may hold values from 1.12896 to 112.896, as said below
- table_first: float32 [16, 169], P('tensor'), may hold values from -20 to 20
- table_second: float32 [16, 169], P('tensor'), may hold values from 0.87808 to 3.7632
Outputs:
- block_out: float32 [12544, 512], P(('dp', 'tensor'))
- grad_in: float32 [12544, 512], P(('dp', 'tensor'))
- qkv_first_new: float32 [3, 512, 512], P(None, 'dp', 'tensor')
- qkv_second_new: float32 [3, 512, 512], P(None, 'dp', 'tensor')
- qkv_new: float32 [3, 512, 512], P(None, 'dp', 'tensor')
- proj_first_new: float32 [512, 512], P('tensor', 'dp')
- proj_second_new: float32 [512, 512], P('tensor', 'dp')
- proj_new: float32 [512, 512], P('tensor', 'dp')
- fc1_first_new: float32 [512, 2048], P('dp', 'tensor')
- fc1_second_new: float32 [512, 2048], P('dp', 'tensor')
- fc1_new: float32 [512, 2048], P('dp', 'tensor')
- fc2_first_new: float32 [2048, 512], P('tensor', 'dp')
- fc2_second_new: float32 [2048, 512], P('tensor', 'dp')
- fc2_new: float32 [2048, 512], P('tensor', 'dp')
- small_first_new: float32 [12, 512], P(None, 'dp')
- small_second_new: float32 [12, 512], P(None, 'dp')
- small_new: float32 [12, 512], P(None, 'dp')
- table_first_new: float32 [16, 169], P('tensor')
- table_second_new: float32 [16, 169], P('tensor')
- table_new: float32 [16, 169], P('tensor')
The draws below stay inside these ranges and needn't reach their ends.
Inputs may be any that keep to these rules, and one draw needn't show every extreme that they name: `small_params`: norm gains near one, other rows of either sign. `small_first`: both signs. `small_second`: positive.
All inputs are finite; a program needn't handle non-finite values.
Results may differ from the reference program's by a relative error of at most 0.015.
The reference program's roundings to bfloat16 on the way count: a program that leaves them out, or rounds other values in their place, can miss the bound.
Values may be sent and summed in bfloat16 or wider, within the bound.
A program may use at most 128 MiB of HBM per device.

```python
import jax
import jax.numpy as jnp
import numpy as np
from jax import lax

C = 512
HEADS = 16
HD = 32
FF = 2048
WIN = 7
SIDE = 14
SHIFT = 3
STEP = 10
TABLE = 169
VROWS = 12
TOKENS = 12544


def row_scales():
    leading = jnp.array([1.5, 1.5, 0.6, 0.6, 0.6, 1.5, 1.2, 1.0], jnp.float32)
    return jnp.concatenate([leading, jnp.full((VROWS - 8,), 0.3, jnp.float32)])[:, None]


def signed_noise(key):
    return jnp.clip(jax.random.normal(key, (VROWS, C), jnp.float32), -4.0, 4.0)


def draw_small_params(key, part):
    key = jax.random.fold_in(key, 11)
    noise_draw = signed_noise(key)
    row_ids = jnp.arange(VROWS)[:, None]
    return jnp.where((row_ids == 0) | (row_ids == 2), 1.0 + 0.15 * noise_draw, 0.3 * noise_draw)


def draw_small_first(key, part):
    key = jax.random.fold_in(key, 12)
    noise_draw = signed_noise(key)
    return noise_draw * 0.11 * row_scales() * TOKENS ** 0.5


def draw_small_second(key, part):
    key = jax.random.fold_in(key, 13)
    factor = jax.random.uniform(key, (VROWS, C), jnp.float32, 1.0, 4.0)
    return factor * 0.001 * row_scales() ** 2 * TOKENS


def spiked(result, rng, source, target, shards_of, factor):
    def block_of(axis_at):
        return (jnp.arange(result.shape[axis_at]) // (result.shape[axis_at] // shards_of)).reshape((-1,) + (1,) * (result.ndim - 1 - axis_at))

    near = jax.random.permutation(rng, shards_of)[block_of(target)]
    other_side = (block_of(target) + shards_of // 2) % shards_of
    return jnp.where((block_of(source) == near) | (block_of(source) == other_side), factor * result, result)


def block_levels(key, shape, shards, low, high):
    level, own = 1.0, jax.random.fold_in(key, 6)
    for axis_at, parts in shards:
        draws = jnp.exp(jax.random.uniform(jax.random.fold_in(own, axis_at), (parts,), jnp.float32, low / len(shards), high / len(shards)))
        level = level * jnp.repeat(draws, shape[axis_at] // parts).reshape([-1 if axis == axis_at else 1 for axis in range(len(shape))])
    return level


def scatter_about(own_key, shape, width, most, shards=(), held_as=jnp.bfloat16):
    drawn = jax.random.normal(own_key, shape, jnp.float32) * width
    if len(shards) > 0:
        drawn = block_levels(own_key, shape, shards, -0.22, 0.18) * drawn
    return jnp.clip(drawn, min=-most, max=most).astype(held_as)


def gaussian_with(key, extent, scale, reach, cuts, heavy, dtype=jnp.bfloat16):
    values = scale * jax.random.normal(key, extent, jnp.float32)
    if cuts:
        values = values * block_levels(key, extent, cuts, -0.22, 0.18)
    return jnp.clip(spiked(values, jax.random.fold_in(key, 3), *heavy), -reach, reach).astype(dtype)


def setup_inputs(seed: int = 0) -> dict:
    keys = jax.random.split(jax.random.key(seed), 21)
    tokens_in = scatter_about(keys[0], (TOKENS, C), 1.0, 6.0, ((0, 32),), jnp.float32)
    out_grad = gaussian_with(keys[1], (TOKENS, C), 1.0, 12.0, ((0, 32),), (0, 1, 32, 2.75), jnp.float32)
    w_qkv = scatter_about(keys[2], (3, C, C), C ** -0.5, 0.25, ((1, 8), (2, 4)), jnp.float32)
    w_proj = scatter_about(keys[3], (C, C), (C // 16) ** -0.5, 1.0, ((0, 4), (1, 8)), jnp.float32)
    w_fc1 = scatter_about(keys[4], (C, FF), C ** -0.5, 0.25, ((0, 8), (1, 4)), jnp.float32)
    w_fc2 = scatter_about(keys[5], (FF, C), FF ** -0.5, 0.125, ((0, 4), (1, 8)), jnp.float32)
    small_params = draw_small_params(jax.random.fold_in(keys[20], 71), 0)
    bias_table = scatter_about(keys[7], (HEADS, TABLE), 1.0, 6.0, ((0, 4),), jnp.float32)
    qkv_first = scatter_about(keys[8], (3, C, C), (0.11 * TOKENS ** 0.5), 80.0, ((1, 8), (2, 4)), jnp.float32)
    qkv_second = jnp.clip(12.544 + 37.632 * jax.random.uniform(keys[9], (3, C, C), jnp.float32) ** block_levels(keys[9], (3, C, C), ((1, 8), (2, 4)), -0.2, 0.2), 12.544, 50.176)
    proj_first = scatter_about(keys[10], (C, C), (0.044 * TOKENS ** 0.5), 32.0, ((0, 4), (1, 8)), jnp.float32)
    proj_second = jnp.clip(2.00704 + 6.02112 * jax.random.uniform(keys[11], (C, C), jnp.float32) ** block_levels(keys[11], (C, C), ((0, 4), (1, 8)), -0.2, 0.2), 2.00704, 8.02816)
    fc1_first = scatter_about(keys[12], (C, FF), (0.033 * TOKENS ** 0.5), 24.0, ((0, 8), (1, 4)), jnp.float32)
    fc1_second = jnp.clip(1.12896 + 3.38688 * jax.random.uniform(keys[13], (C, FF), jnp.float32) ** block_levels(keys[13], (C, FF), ((0, 8), (1, 4)), -0.2, 0.2), 1.12896, 4.51584)
    fc2_first = scatter_about(keys[14], (FF, C), (0.072 * TOKENS ** 0.5), 48.0, ((0, 4), (1, 8)), jnp.float32)
    fc2_second = jnp.clip(5.26848 + 16.05632 * jax.random.uniform(keys[15], (FF, C), jnp.float32) ** block_levels(keys[15], (FF, C), ((0, 4), (1, 8)), -0.2, 0.2), 5.26848, 21.3248)
    small_first = draw_small_first(jax.random.fold_in(keys[20], 71), 0)
    small_second = draw_small_second(jax.random.fold_in(keys[20], 71), 0)
    table_first = scatter_about(keys[18], (HEADS, TABLE), (0.03 * TOKENS ** 0.5), 20.0, ((0, 4),), jnp.float32)
    table_second = jnp.clip(0.87808 + 2.88512 * jax.random.uniform(keys[19], (HEADS, TABLE), jnp.float32) ** block_levels(keys[19], (HEADS, TABLE), ((0, 4),), -0.2, 0.2), 0.87808, 3.7632)
    return {"tokens_in": tokens_in, "out_grad": out_grad, "w_qkv": w_qkv, "w_proj": w_proj, "w_fc1": w_fc1, "w_fc2": w_fc2, "small_params": small_params, "bias_table": bias_table, "qkv_first": qkv_first, "qkv_second": qkv_second, "proj_first": proj_first, "proj_second": proj_second, "fc1_first": fc1_first, "fc1_second": fc1_second, "fc2_first": fc2_first, "fc2_second": fc2_second, "small_first": small_first, "small_second": small_second, "table_first": table_first, "table_second": table_second}


@jax.custom_vjp
def low(v):
    return lax.optimization_barrier(v.astype(jnp.bfloat16)).astype(jnp.float32)

@jax.custom_vjp
def low_back(v):
    return v

def low_keep(v):
    return (low(v), None)

def low_pass(kept, grad):
    return (grad,)

def back_keep(v):
    return (v, None)

def back_low(kept, grad):
    return (low(grad),)
low.defvjp(low_keep, low_pass)
low_back.defvjp(back_keep, back_low)
norm_eps = 1e-05
mask_fill = -100.0
beta_one = 0.9
beta_two = 0.999
adam_eps = 1e-08
weight_decay = 0.05
rate_matrix = 0.1
rate_small = 1.0

def region_label(position, image_side, win_side, shift_by):
    return np.where(position < image_side - win_side, 0, np.where(position < image_side - shift_by, 1, 2))

def window_tables(win_side, image_side, shift_by):
    cell_total = win_side * win_side
    cell_rows = np.arange(cell_total) // win_side
    cell_cols = np.arange(cell_total) % win_side
    index_table = (cell_rows[:, None] - cell_rows[None, :] + win_side - 1) * (2 * win_side - 1) + (cell_cols[:, None] - cell_cols[None, :] + win_side - 1)
    per_side = image_side // win_side
    mask_list = []
    for window_row in range(per_side):
        for window_col in range(per_side):
            label_rows = region_label(window_row * win_side + cell_rows, image_side, win_side, shift_by)
            label_cols = region_label(window_col * win_side + cell_cols, image_side, win_side, shift_by)
            labels = 3 * label_rows + label_cols
            mask_list.append(np.where(labels[:, None] != labels[None, :], mask_fill, 0.0))
    return (index_table, np.stack(mask_list).astype(np.float32))

def layer_norm(values):
    center = values - lax.optimization_barrier(jnp.mean(values, axis=-1, keepdims=True))
    spread = lax.rsqrt(lax.optimization_barrier(jnp.mean(center * center, axis=-1, keepdims=True)) + norm_eps)
    return center * spread

def to_windows(flat_rows):
    images = flat_rows.shape[0] // (SIDE * SIDE)
    channels = flat_rows.shape[1]
    per_side = SIDE // WIN
    lattice = jnp.roll(flat_rows.reshape(images, SIDE, SIDE, channels), (-SHIFT, -SHIFT), (1, 2))
    lattice = lattice.reshape(images, per_side, WIN, per_side, WIN, channels).transpose(0, 1, 3, 2, 4, 5)
    return lattice.reshape(flat_rows.shape[0], channels)

def from_windows(flat_rows):
    images = flat_rows.shape[0] // (SIDE * SIDE)
    channels = flat_rows.shape[1]
    per_side = SIDE // WIN
    lattice = flat_rows.reshape(images, per_side, per_side, WIN, WIN, channels).transpose(0, 1, 3, 2, 4, 5)
    lattice = jnp.roll(lattice.reshape(images, SIDE, SIDE, channels), (SHIFT, SHIFT), (1, 2))
    return lattice.reshape(flat_rows.shape[0], channels)

def exact_dot(left, right):
    return jnp.dot(left, right, precision=lax.Precision.HIGHEST)

def forward(tokens_in, w_qkv, w_proj, w_fc1, w_fc2, small_params, bias_table):
    index_table, mask_table = window_tables(WIN, SIDE, SHIFT)
    weight_qkv = low(w_qkv)
    weight_proj = low(w_proj)
    weight_one = low(w_fc1)
    weight_two = low(w_fc2)
    small_low = low(small_params)
    table_low = low(bias_table)
    row_count = tokens_in.shape[0]
    act_low = low(layer_norm(tokens_in) * small_low[0] + small_low[1])
    act_win = to_windows(act_low)
    queries = low(low_back(exact_dot(act_win, weight_qkv[0]) + small_low[4]))
    key_rows = low(low_back(exact_dot(act_win, weight_qkv[1])))
    val_rows = low(low_back(exact_dot(act_win, weight_qkv[2]) + small_low[5]))
    windows = row_count // (WIN * WIN)
    block_shape = (windows, WIN * WIN, HEADS, HD)
    scores = jnp.einsum('wihd,wjhd->whij', queries.reshape(block_shape), key_rows.reshape(block_shape), precision=lax.Precision.HIGHEST) * HD ** (-0.5)
    bias_grid = table_low[:, index_table]
    per_image = (SIDE // WIN) ** 2
    mask_all = jnp.asarray(np.tile(mask_table, (windows // per_image, 1, 1)))
    scores = low_back(scores + bias_grid[None] + mask_all[:, None])
    probs = low(jax.nn.softmax(scores, axis=-1))
    attn = jnp.einsum('whij,wjhd->wihd', probs, val_rows.reshape(block_shape), precision=lax.Precision.HIGHEST).reshape(row_count, C)
    attn_tok = from_windows(low(low_back(attn)))
    middle = tokens_in + low_back(exact_dot(attn_tok, weight_proj) + small_low[6])
    mixed = low(layer_norm(middle) * small_low[2] + small_low[3])
    hidden = low_back(exact_dot(mixed, weight_one) + small_low[8:].reshape(FF))
    gelu_out = low(jax.nn.gelu(hidden, approximate=False))
    return middle + low_back(exact_dot(gelu_out, weight_two) + small_low[7])

def adam_update(weight, grad, first, second, rate):
    first_new = beta_one * first + (1.0 - beta_one) * grad
    second_new = beta_two * second + (1.0 - beta_two) * grad * grad
    first_hat = first_new / (1.0 - beta_one ** STEP)
    second_hat = second_new / (1.0 - beta_two ** STEP)
    weight_new = weight - rate * (first_hat / (jnp.sqrt(second_hat) + adam_eps) + weight_decay * weight)
    return (first_new, second_new, weight_new)

def reference(tokens_in, out_grad, w_qkv, w_proj, w_fc1, w_fc2, small_params, bias_table, qkv_first, qkv_second, proj_first, proj_second, fc1_first, fc1_second, fc2_first, fc2_second, small_first, small_second, table_first, table_second):
    group_rows = 4 * SIDE * SIDE
    groups = tokens_in.shape[0] // group_rows
    weights = (w_qkv, w_proj, w_fc1, w_fc2, small_params, bias_table)

    def step_group(running, inputs_pair):
        piece_in, piece_grad = inputs_pair
        out_rows, pullback = jax.vjp(forward, piece_in, *weights)
        grads = pullback(piece_grad)
        totals = jax.tree.map(lambda total_sum, added: total_sum + added, running, tuple(grads[1:]))
        return (totals, (out_rows, grads[0]))
    initial = jax.tree.map(jnp.zeros_like, weights)
    totals, (outputs, grad_rows) = lax.scan(step_group, initial, (tokens_in.reshape(groups, group_rows, C), out_grad.reshape(groups, group_rows, C)))
    grad_qkv, grad_proj, grad_one, grad_two, grad_small, grad_table = totals
    qkv_first_new, qkv_second_new, qkv_new = adam_update(w_qkv, grad_qkv, qkv_first, qkv_second, rate_matrix)
    proj_first_new, proj_second_new, proj_new = adam_update(w_proj, grad_proj, proj_first, proj_second, rate_matrix)
    fc1_first_new, fc1_second_new, fc1_new = adam_update(w_fc1, grad_one, fc1_first, fc1_second, rate_matrix)
    fc2_first_new, fc2_second_new, fc2_new = adam_update(w_fc2, grad_two, fc2_first, fc2_second, rate_matrix)
    small_first_new, small_second_new, small_new = adam_update(small_params, grad_small, small_first, small_second, rate_small)
    table_first_new, table_second_new, table_new = adam_update(bias_table, grad_table, table_first, table_second, rate_small)
    return (outputs.reshape(TOKENS, C), grad_rows.reshape(TOKENS, C), qkv_first_new, qkv_second_new, qkv_new, proj_first_new, proj_second_new, proj_new, fc1_first_new, fc1_second_new, fc1_new, fc2_first_new, fc2_second_new, fc2_new, small_first_new, small_second_new, small_new, table_first_new, table_second_new, table_new)
```

```python
import functools
import math

import jax
import jax.numpy as jnp
import numpy as np
from jax import lax
from jax.experimental import pallas as pl
from jax.experimental.pallas import tpu as pltpu
from jax.sharding import PartitionSpec as P

FF = 2048
WIN = 7
SIDE = 14
SHIFT = 3
STEP = 10


norm_eps = 1e-05
mask_fill = -100.0
beta_one = 0.9
beta_two = 0.999
adam_eps = 1e-08
weight_decay = 0.05
rate_matrix = 0.1
rate_small = 1.0
inv_root_two = 1.0 / math.sqrt(2.0)
inv_root_tau = 1.0 / math.sqrt(2.0 * math.pi)


def axis_bits(size):
    return size.bit_length() - 1


def bit_orders(dp_size, tensor_size):
    dp_bits = [("dp", bit) for bit in reversed(range(axis_bits(dp_size)))]
    tensor_bits = [("tensor", bit) for bit in reversed(range(axis_bits(tensor_size)))]
    if dp_size == 8 and tensor_size == 4:
        z_high, z_low, x_bit = dp_bits
        y_bit, core = tensor_bits
        return (
            (z_high, z_low, x_bit, y_bit, core),
            (z_high, z_low, y_bit, x_bit, core),
            (x_bit, y_bit, z_high, z_low, core),
        )
    core = dp_bits[-1]
    rest = dp_bits[:-1]
    return (
        tuple(rest + tensor_bits + [core]),
        tuple(rest + tensor_bits + [core]),
        tuple(tensor_bits + rest + [core]),
    )


def bit_value(place, bit):
    axis, level = bit
    return (place[axis] // (2**level)) % 2


def slot_of(place, order):
    slot = 0
    for level, bit in enumerate(order):
        slot = slot + bit_value(place, bit) * (2**level)
    return slot


def partner_of(place, bit):
    axis, level = bit
    other = place[axis] + (1 - 2 * bit_value(place, bit)) * (2**level)
    return tuple(other if name == axis else place[name] for name in ("dp", "tensor"))


def greet(place, order):
    barrier = pltpu.get_barrier_semaphore()
    for bit in order:
        pl.semaphore_signal(
            barrier, inc=1, device_id=partner_of(place, bit), device_id_type=pl.DeviceIdType.MESH
        )
    pl.semaphore_wait(barrier, len(order))


def here():
    return {"dp": lax.axis_index("dp"), "tensor": lax.axis_index("tensor")}


def gather_kernel(orders, *refs):
    parts = len(orders)
    ins, outs = refs[:parts], refs[parts : 2 * parts]
    send_sem, recv_sem, own_sem = refs[2 * parts :]
    place = here()
    stages = len(orders[0])
    greet(place, orders[0])
    slots = [slot_of(place, order) for order in orders]
    own_copies = []
    for part in range(parts):
        own = pltpu.make_async_copy(ins[part], outs[part].at[slots[part]], own_sem.at[part])
        own.start()
        own_copies.append(own)
    copies = {}
    for stage in range(stages):
        for part in range(parts):
            if stage == 0:
                source, target = ins[part], outs[part].at[slots[part]]
            else:
                if stage == 1:
                    own_copies[part].wait()
                copies[part, stage - 1].wait_recv()
                first = (slots[part] // (2**stage)) * (2**stage)
                source = target = outs[part].at[pl.ds(first, 2**stage)]
            copy = pltpu.make_async_remote_copy(
                src_ref=source,
                dst_ref=target,
                send_sem=send_sem.at[part, stage],
                recv_sem=recv_sem.at[part, stage],
                device_id=partner_of(place, orders[part][stage]),
                device_id_type=pl.DeviceIdType.MESH,
            )
            copy.start()
            copies[part, stage] = copy
    for part in range(parts):
        copies[part, stages - 1].wait_recv()
    for copy in copies.values():
        copy.wait_send()


def gather_blocks(blocks, orders):
    stages = len(orders[0])
    parts = len(blocks)
    return pl.pallas_call(
        functools.partial(gather_kernel, orders),
        out_shape=[jax.ShapeDtypeStruct((2**stages,) + b.shape, b.dtype) for b in blocks],
        in_specs=[pl.BlockSpec(memory_space=pl.ANY)] * parts,
        out_specs=[pl.BlockSpec(memory_space=pl.ANY)] * parts,
        scratch_shapes=[
            pltpu.SemaphoreType.DMA((parts, stages)),
            pltpu.SemaphoreType.DMA((parts, stages)),
            pltpu.SemaphoreType.DMA((parts,)),
        ],
        compiler_params=pltpu.CompilerParams(collective_id=1, has_side_effects=True),
        name="gather_weights",
    )(*blocks)


def reduce_kernel(orders, *refs):
    parts = len(orders)
    ins, small_in = refs[:parts], refs[parts]
    outs, small_out = refs[parts + 1 : 2 * parts + 1], refs[2 * parts + 1]
    rest = refs[2 * parts + 2 :]
    accs, recvs = rest[:parts], rest[parts : 2 * parts]
    small_acc, small_recv, send_sem, recv_sem = rest[2 * parts :]
    place = here()
    stages = len(orders[0])
    slots = [slot_of(place, order) for order in orders]
    greet(place, orders[0])
    small_acc[0] = small_in[...]
    copies = {}

    def send(part, stage):
        order = orders[part] if part < parts else orders[0]
        bit = order[stages - 1 - stage]
        half = 2 ** (stages - 1 - stage)
        if part == parts:
            source, target = small_acc.at[stage], small_recv.at[stage]
        else:
            mine = bit_value(place, bit)
            source = (ins[part] if stage == 0 else accs[part]).at[pl.ds((1 - mine) * half, half)]
            target = recvs[part].at[pl.ds(half, half)]
        copy = pltpu.make_async_remote_copy(
            src_ref=source,
            dst_ref=target,
            send_sem=send_sem.at[part, stage],
            recv_sem=recv_sem.at[part, stage],
            device_id=partner_of(place, bit),
            device_id_type=pl.DeviceIdType.MESH,
        )
        copy.start()
        copies[part, stage] = copy

    for part in range(parts + 1):
        send(part, 0)
    for stage in range(stages):
        half = 2 ** (stages - 1 - stage)
        for part in range(parts + 1):
            copies[part, stage].wait_recv()
            if part == parts:
                small_acc[stage + 1] = small_acc[stage] + small_recv[stage]
            else:
                mine = bit_value(place, orders[part][stages - 1 - stage])
                source = ins[part] if stage == 0 else accs[part]
                if stage > 0:
                    copies[part, stage].wait_send()

                def add(index, carry):
                    total = source[mine * half + index].astype(jnp.float32) + recvs[part][
                        half + index
                    ].astype(jnp.float32)
                    if stage == stages - 1:
                        outs[part][...] = total
                    else:
                        accs[part][index] = total.astype(jnp.bfloat16)
                    return carry

                lax.fori_loop(0, half, add, 0)
            if stage < stages - 1:
                send(part, stage + 1)
    small_out[...] = small_acc[stages]
    for (part, stage), copy in copies.items():
        if part == parts or stage == 0:
            copy.wait_send()


def reduce_blocks(blocks, small, orders):
    stages = len(orders[0])
    parts = len(blocks)
    count = 2**stages
    vmem = pl.BlockSpec(memory_space=pltpu.VMEM)
    return pl.pallas_call(
        functools.partial(reduce_kernel, orders),
        out_shape=[jax.ShapeDtypeStruct(b.shape[1:], jnp.float32) for b in blocks]
        + [jax.ShapeDtypeStruct(small.shape, jnp.float32)],
        in_specs=[vmem] * (parts + 1),
        out_specs=[vmem] * (parts + 1),
        scratch_shapes=[pltpu.VMEM((count // 2,) + b.shape[1:], jnp.bfloat16) for b in blocks]
        + [pltpu.VMEM(b.shape, jnp.bfloat16) for b in blocks]
        + [
            pltpu.VMEM((stages + 1,) + small.shape, jnp.float32),
            pltpu.VMEM((stages,) + small.shape, jnp.float32),
            pltpu.SemaphoreType.DMA((parts + 1, stages)),
            pltpu.SemaphoreType.DMA((parts + 1, stages)),
        ],
        compiler_params=pltpu.CompilerParams(
            collective_id=2, has_side_effects=True, vmem_limit_bytes=40 * 2**20
        ),
        name="reduce_gradients",
    )(*blocks, small)


def mesh_bits(dp_size, tensor_size):
    return [("dp", bit) for bit in reversed(range(axis_bits(dp_size)))] + [
        ("tensor", bit) for bit in reversed(range(axis_bits(tensor_size)))
    ]


def to_mesh_order(gathered, order, dp_size, tensor_size):
    slot_bits = list(reversed(order))
    wanted = mesh_bits(dp_size, tensor_size)
    count = len(wanted)
    tail = gathered.shape[1:]
    split = gathered.reshape((2,) * count + tail)
    axes = [slot_bits.index(bit) for bit in wanted] + [count + i for i in range(len(tail))]
    return split.transpose(axes).reshape((dp_size, tensor_size) + tail)


def to_slot_order(values, order, dp_size, tensor_size):
    slot_bits = list(reversed(order))
    held = mesh_bits(dp_size, tensor_size)
    count = len(held)
    tail = values.shape[2:]
    split = values.reshape((2,) * count + tail)
    axes = [held.index(bit) for bit in slot_bits] + [count + i for i in range(len(tail))]
    return split.transpose(axes).reshape((2**count,) + tail)


def wide(block):
    rows, columns = block.shape[-2:]
    if rows % 16 == 0:
        return block
    return block.reshape(block.shape[:-2] + (rows * 2, columns // 2))


def region_label(position, image_side, win_side, shift_by):
    return np.where(
        position < image_side - win_side, 0, np.where(position < image_side - shift_by, 1, 2)
    )


def window_tables(win_side, image_side, shift_by):
    cell_total = win_side * win_side
    cell_rows = np.arange(cell_total) // win_side
    cell_cols = np.arange(cell_total) % win_side
    index_table = (cell_rows[:, None] - cell_rows[None, :] + win_side - 1) * (2 * win_side - 1) + (
        cell_cols[:, None] - cell_cols[None, :] + win_side - 1
    )
    per_side = image_side // win_side
    mask_list = []
    for window_row in range(per_side):
        for window_col in range(per_side):
            label_rows = region_label(
                window_row * win_side + cell_rows, image_side, win_side, shift_by
            )
            label_cols = region_label(
                window_col * win_side + cell_cols, image_side, win_side, shift_by
            )
            labels = 3 * label_rows + label_cols
            mask_list.append(np.where(labels[:, None] != labels[None, :], mask_fill, 0.0))
    return (index_table, np.stack(mask_list).astype(np.float32))


def layer_norm(values):
    center = values - jnp.mean(values, axis=-1, keepdims=True)
    spread = lax.rsqrt(jnp.mean(center * center, axis=-1, keepdims=True) + norm_eps)
    return (center * spread, spread)


def norm_back(grad_norm, normed, spread, gain):
    scaled = grad_norm * gain
    return spread * (
        scaled
        - jnp.mean(scaled, axis=-1, keepdims=True)
        - normed * jnp.mean(scaled * normed, axis=-1, keepdims=True)
    )


def to_windows(flat_rows):
    images = flat_rows.shape[0] // (SIDE * SIDE)
    channels = flat_rows.shape[1]
    per_side = SIDE // WIN
    lattice = jnp.roll(flat_rows.reshape(images, SIDE, SIDE, channels), (-SHIFT, -SHIFT), (1, 2))
    lattice = lattice.reshape(images, per_side, WIN, per_side, WIN, channels).transpose(
        0, 1, 3, 2, 4, 5
    )
    return lattice.reshape(flat_rows.shape[0], channels)


def from_windows(flat_rows):
    images = flat_rows.shape[0] // (SIDE * SIDE)
    channels = flat_rows.shape[1]
    per_side = SIDE // WIN
    lattice = flat_rows.reshape(images, per_side, per_side, WIN, WIN, channels).transpose(
        0, 1, 3, 2, 4, 5
    )
    lattice = jnp.roll(lattice.reshape(images, SIDE, SIDE, channels), (SHIFT, SHIFT), (1, 2))
    return lattice.reshape(flat_rows.shape[0], channels)


def window_scores(queries, key_rows, bias_grid, mask_grid, score_scale):
    scores = (
        jnp.einsum("wihd,wjhd->whij", queries, key_rows, preferred_element_type=jnp.float32)
        * score_scale
    )
    return scores + bias_grid[None] + mask_grid[:, None]


def attend(queries, key_rows, val_rows, bias_grid, mask_grid, score_scale):
    scores = window_scores(queries, key_rows, bias_grid, mask_grid, score_scale)
    highest = jnp.max(scores, axis=-1, keepdims=True)
    exp_terms = jnp.exp(scores - highest)
    totals = jnp.sum(exp_terms, axis=-1, keepdims=True)
    probs = (exp_terms / totals).astype(jnp.bfloat16)
    output = jnp.einsum("whij,wjhd->wihd", probs, val_rows, preferred_element_type=jnp.float32)
    return (output.astype(jnp.bfloat16), (highest + jnp.log(totals))[..., 0])


def attend_back(
    queries, key_rows, val_rows, grad_attn, log_total, bias_grid, mask_grid, score_scale
):
    scores = window_scores(queries, key_rows, bias_grid, mask_grid, score_scale)
    probs = jnp.exp(scores - log_total[..., None])
    grad_probs = jnp.einsum(
        "wihd,wjhd->whij", grad_attn, val_rows, preferred_element_type=jnp.float32
    )
    inner_sum = jnp.sum(probs * grad_probs, axis=-1, keepdims=True)
    grad_scores = (probs * (grad_probs - inner_sum)).astype(jnp.bfloat16)
    grad_query = (
        jnp.einsum("whij,wjhd->wihd", grad_scores, key_rows, preferred_element_type=jnp.float32)
        * score_scale
    ).astype(jnp.bfloat16)
    grad_key = (
        jnp.einsum("whij,wihd->wjhd", grad_scores, queries, preferred_element_type=jnp.float32)
        * score_scale
    ).astype(jnp.bfloat16)
    grad_value = jnp.einsum(
        "whij,wihd->wjhd", probs.astype(jnp.bfloat16), grad_attn, preferred_element_type=jnp.float32
    ).astype(jnp.bfloat16)
    grad_bias = jnp.sum(grad_scores.astype(jnp.float32), axis=0)
    return (grad_query, grad_key, grad_value, grad_bias)


def run_block(
    tokens_in,
    out_grad,
    w_qkv,
    wt_proj,
    w_fc1,
    wt_fc2,
    small_all,
    table_low,
):
    row_count = tokens_in.shape[0]
    channels = tokens_in.shape[1]
    heads_here = table_low.shape[0]
    head_cols = wt_proj.shape[1]
    head_size = head_cols // heads_here
    score_scale = head_size ** (-0.5)
    small_vals = small_all.astype(jnp.float32)
    gain_one = small_vals[0]
    bias_one = small_vals[1]
    gain_two = small_vals[2]
    bias_two = small_vals[3]
    bias_query = small_vals[4]
    bias_value = small_vals[5]
    bias_proj = small_vals[6]
    bias_out = small_vals[7]
    bias_hidden = small_vals[8:].reshape(-1)
    index_table, mask_table = window_tables(WIN, SIDE, SHIFT)
    table_size = (2 * WIN - 1) ** 2
    cell_count = WIN * WIN
    lookup = jnp.asarray(
        (index_table.reshape(-1)[:, None] == np.arange(table_size)[None, :]).astype(np.float32)
    )
    bias_grid = lax.dot_general(
        table_low.astype(jnp.float32),
        lookup,
        (((1,), (1,)), ((), ())),
        precision=lax.Precision.HIGHEST,
    ).reshape(heads_here, cell_count, cell_count)
    normed_one, spread_one = layer_norm(tokens_in)
    act_low = (normed_one * gain_one + bias_one).astype(jnp.bfloat16)
    act_all = act_low
    all_rows = act_all.shape[0]
    act_win = to_windows(act_all)
    projected = jnp.einsum("rc,kcd->krd", act_win, w_qkv, preferred_element_type=jnp.float32)
    queries = (projected[0] + bias_query).astype(jnp.bfloat16)
    key_rows = projected[1].astype(jnp.bfloat16)
    val_rows = (projected[2] + bias_value).astype(jnp.bfloat16)
    windows = all_rows // cell_count
    block_windows = math.gcd(windows, 16)
    per_image = (SIDE // WIN) ** 2
    mask_grid = jnp.asarray(np.tile(mask_table, (block_windows // per_image, 1, 1)))
    block_shape = (windows // block_windows, block_windows, cell_count, heads_here, head_size)
    query_blocks = queries.reshape(block_shape)
    key_blocks = key_rows.reshape(block_shape)
    value_blocks = val_rows.reshape(block_shape)
    attn_blocks, log_totals = lax.map(
        lambda packed: attend(packed[0], packed[1], packed[2], bias_grid, mask_grid, score_scale),
        (query_blocks, key_blocks, value_blocks),
    )
    attn_tok = from_windows(attn_blocks.reshape(all_rows, head_cols))
    proj_sum = lax.dot_general(
        attn_tok, wt_proj, (((1,), (1,)), ((), ())), preferred_element_type=jnp.float32
    )
    middle = tokens_in + proj_sum + bias_proj
    normed_two, spread_two = layer_norm(middle)
    mixed = (normed_two * gain_two + bias_two).astype(jnp.bfloat16)
    mixed_all = mixed
    hidden = jnp.dot(mixed_all, w_fc1, preferred_element_type=jnp.float32) + bias_hidden
    gelu_out = jax.nn.gelu(hidden, approximate=False).astype(jnp.bfloat16)
    mlp_sum = lax.dot_general(
        gelu_out, wt_fc2, (((1,), (1,)), ((), ())), preferred_element_type=jnp.float32
    )
    result = middle + mlp_sum + bias_out
    grad_low = out_grad.astype(jnp.bfloat16)
    grad_all = grad_low
    grad_w2 = lax.dot_general(
        grad_all, gelu_out, (((0,), (0,)), ((), ())), preferred_element_type=jnp.float32
    )
    grad_gelu = lax.dot_general(
        grad_all, wt_fc2, (((1,), (0,)), ((), ())), preferred_element_type=jnp.float32
    )
    slope = (
        0.5 * (1.0 + lax.erf(hidden * inv_root_two))
        + hidden * jnp.exp(-0.5 * hidden * hidden) * inv_root_tau
    )
    grad_hidden = (grad_gelu * slope).astype(jnp.bfloat16)
    grad_w1 = lax.dot_general(
        mixed_all, grad_hidden, (((0,), (0,)), ((), ())), preferred_element_type=jnp.float32
    )
    grad_bias_hidden = jnp.sum(grad_hidden.astype(jnp.float32), axis=0)
    grad_mixed = lax.dot_general(
        grad_hidden, w_fc1, (((1,), (1,)), ((), ())), preferred_element_type=jnp.float32
    )
    grad_gain_two = jnp.sum(grad_mixed * normed_two, axis=0)
    grad_bias_two = jnp.sum(grad_mixed, axis=0)
    grad_middle = out_grad + norm_back(grad_mixed, normed_two, spread_two, gain_two)
    grad_branch = grad_middle.astype(jnp.bfloat16)
    grad_branch_all = grad_branch
    grad_wp = lax.dot_general(
        grad_branch_all, attn_tok, (((0,), (0,)), ((), ())), preferred_element_type=jnp.float32
    )
    grad_attn = lax.dot_general(
        grad_branch_all, wt_proj, (((1,), (0,)), ((), ())), preferred_element_type=jnp.float32
    ).astype(jnp.bfloat16)
    grad_attn_blocks = to_windows(grad_attn).reshape(block_shape)
    grad_query, grad_key, grad_value, grad_bias = lax.map(
        lambda packed: attend_back(
            packed[0], packed[1], packed[2], packed[3], packed[4], bias_grid, mask_grid, score_scale
        ),
        (query_blocks, key_blocks, value_blocks, grad_attn_blocks, log_totals),
    )
    grad_stack = jnp.stack(
        [
            grad_query.reshape(all_rows, head_cols),
            grad_key.reshape(all_rows, head_cols),
            grad_value.reshape(all_rows, head_cols),
        ],
        axis=1,
    )
    grad_wqkv = jnp.einsum("rc,rkd->kcd", act_win, grad_stack, preferred_element_type=jnp.float32)
    grad_bias_query = jnp.sum(grad_stack[:, 0].astype(jnp.float32), axis=0)
    grad_bias_value = jnp.sum(grad_stack[:, 2].astype(jnp.float32), axis=0)
    grad_stack_tok = from_windows(grad_stack.reshape(all_rows, 3 * head_cols)).reshape(
        all_rows, 3, head_cols
    )
    grad_act = jnp.einsum(
        "rkd,kcd->rc", grad_stack_tok, w_qkv, preferred_element_type=jnp.float32
    )
    grad_gain_one = jnp.sum(grad_act * normed_one, axis=0)
    grad_bias_one = jnp.sum(grad_act, axis=0)
    grad_tokens = grad_middle + norm_back(grad_act, normed_one, spread_one, gain_one)
    grad_bias_proj = jnp.sum(grad_branch.astype(jnp.float32), axis=0)
    grad_bias_out = jnp.sum(grad_low.astype(jnp.float32), axis=0)
    grad_table = lax.dot_general(
        jnp.sum(grad_bias, axis=0).reshape(heads_here, cell_count * cell_count),
        lookup,
        (((1,), (0,)), ((), ())),
        precision=lax.Precision.HIGHEST,
    )
    leading_rows = jnp.stack(
        [
            grad_gain_one,
            grad_bias_one,
            grad_gain_two,
            grad_bias_two,
            grad_bias_query,
            grad_bias_value,
            grad_bias_proj,
            grad_bias_out,
        ]
    )
    small_grad = jnp.concatenate(
        [leading_rows, grad_bias_hidden.reshape(FF // channels, channels)], axis=0
    )
    return (result, grad_tokens, (grad_wqkv, grad_wp, grad_w1, grad_w2, small_grad, grad_table))


def adam_update(weight, grad, first, second, rate):
    first_new = beta_one * first + (1.0 - beta_one) * grad
    second_new = beta_two * second + (1.0 - beta_two) * grad * grad
    first_hat = first_new / (1.0 - beta_one**STEP)
    second_hat = second_new / (1.0 - beta_two**STEP)
    weight_new = weight - rate * (
        first_hat / (jnp.sqrt(second_hat) + adam_eps) + weight_decay * weight
    )
    return (first_new, second_new, weight_new)


def per_device(
    tokens_in,
    out_grad,
    w_qkv,
    w_proj,
    w_fc1,
    w_fc2,
    small_params,
    bias_table,
    qkv_first,
    qkv_second,
    proj_first,
    proj_second,
    fc1_first,
    fc1_second,
    fc2_first,
    fc2_second,
    small_first,
    small_second,
    table_first,
    table_second,
):
    dp_size, tensor_size = lax.axis_size("dp"), lax.axis_size("tensor")
    orders = bit_orders(dp_size, tensor_size)
    rows, head_cols = w_qkv.shape[1:]
    hidden_cols = w_fc1.shape[1]
    channels = tokens_in.shape[1]
    small_rows = small_params.shape[0]
    heads_here, table_size = bias_table.shape
    block_attn = jnp.concatenate([w_qkv, w_proj.T[None]], axis=0).astype(jnp.bfloat16)
    block_attn = block_attn.reshape(4 * rows, head_cols)
    block_one = wide(w_fc1.astype(jnp.bfloat16))
    block_two = wide(w_fc2.T.astype(jnp.bfloat16))
    table_wide = jnp.pad(bias_table, ((0, 0), (0, 256 - table_size))).reshape(-1, 128)
    block_small = jnp.concatenate(
        [
            jnp.pad(small_params, ((0, 16 - small_rows), (0, 128 - rows))),
            jnp.pad(table_wide, ((0, 16 - table_wide.shape[0]), (0, 0))),
        ],
        axis=0,
    ).astype(jnp.bfloat16)
    gathered = gather_blocks(
        (block_attn, block_one, block_two, block_small), orders + (orders[0],)
    )
    all_attn, all_one, all_two, all_small = (
        to_mesh_order(values, order, dp_size, tensor_size)
        for values, order in zip(gathered, orders + (orders[0],))
    )
    all_attn = all_attn.reshape(dp_size, tensor_size, 4, rows, head_cols)
    all_attn = all_attn.transpose(2, 0, 3, 1, 4).reshape(4, channels, channels)
    all_one, all_two = (
        values.reshape(dp_size, tensor_size, rows, hidden_cols)
        .transpose(0, 2, 1, 3)
        .reshape(channels, FF)
        for values in (all_one, all_two)
    )
    small_all = all_small[:, 0, :small_rows, :rows].transpose(1, 0, 2)
    small_all = small_all.reshape(small_rows, channels)
    table_low = all_small[0, :, 16 : 16 + table_wide.shape[0]]
    table_low = table_low.reshape(tensor_size * heads_here, 256)[:, :table_size]
    result, grad_tokens, grads = run_block(
        tokens_in,
        out_grad,
        all_attn[:3],
        all_attn[3],
        all_one,
        all_two,
        small_all,
        table_low,
    )
    grad_wqkv, grad_wp, grad_w1, grad_w2, small_grad, grad_table = grads
    pack_attn = jnp.concatenate([grad_wqkv, grad_wp[None]], axis=0).astype(jnp.bfloat16)
    pack_attn = pack_attn.reshape(4, dp_size, rows, tensor_size, head_cols)
    pack_attn = pack_attn.transpose(1, 3, 0, 2, 4)
    pack_attn = pack_attn.reshape(dp_size, tensor_size, 4 * rows, head_cols)
    pack_one, pack_two = (
        wide(
            values.astype(jnp.bfloat16)
            .reshape(dp_size, rows, tensor_size, hidden_cols)
            .transpose(0, 2, 1, 3)
        )
        for values in (grad_w1, grad_w2)
    )
    packs = tuple(
        to_slot_order(values, order, dp_size, tensor_size)
        for values, order in zip((pack_attn, pack_one, pack_two), orders)
    )
    small_flat = small_grad.reshape(-1, 128)
    pack_small = jnp.concatenate(
        [small_flat, jnp.pad(grad_table, ((0, 0), (0, 256 - table_size))).reshape(-1, 128)], axis=0
    )
    sum_attn, sum_one, sum_two, sum_small = reduce_blocks(packs, pack_small, orders)
    sum_attn = sum_attn.reshape(4, rows, head_cols)
    shard_qkv, shard_proj = sum_attn[:3], sum_attn[3].T
    shard_one = sum_one.reshape(rows, hidden_cols)
    shard_two = sum_two.reshape(rows, hidden_cols).T
    small_total = sum_small[: small_flat.shape[0]].reshape(small_rows, channels)
    shard_small = lax.dynamic_slice_in_dim(small_total, lax.axis_index("dp") * rows, rows, 1)
    table_total = sum_small[small_flat.shape[0] :].reshape(-1, 256)[:, :table_size]
    table_grad = lax.dynamic_slice_in_dim(
        table_total, lax.axis_index("tensor") * heads_here, heads_here, 0
    )
    qkv_first_new, qkv_second_new, qkv_new = adam_update(
        w_qkv, shard_qkv, qkv_first, qkv_second, rate_matrix
    )
    proj_first_new, proj_second_new, proj_new = adam_update(
        w_proj, shard_proj, proj_first, proj_second, rate_matrix
    )
    fc1_first_new, fc1_second_new, fc1_new = adam_update(
        w_fc1, shard_one, fc1_first, fc1_second, rate_matrix
    )
    fc2_first_new, fc2_second_new, fc2_new = adam_update(
        w_fc2, shard_two, fc2_first, fc2_second, rate_matrix
    )
    small_first_new, small_second_new, small_new = adam_update(
        small_params, shard_small, small_first, small_second, rate_small
    )
    table_first_new, table_second_new, table_new = adam_update(
        bias_table, table_grad, table_first, table_second, rate_small
    )
    return (
        result,
        grad_tokens,
        qkv_first_new,
        qkv_second_new,
        qkv_new,
        proj_first_new,
        proj_second_new,
        proj_new,
        fc1_first_new,
        fc1_second_new,
        fc1_new,
        fc2_first_new,
        fc2_second_new,
        fc2_new,
        small_first_new,
        small_second_new,
        small_new,
        table_first_new,
        table_second_new,
        table_new,
    )


def solution(mesh):
    in_specs = (
        P(("dp", "tensor"), None),
        P(("dp", "tensor"), None),
        P(None, "dp", "tensor"),
        P("tensor", "dp"),
        P("dp", "tensor"),
        P("tensor", "dp"),
        P(None, "dp"),
        P("tensor", None),
        P(None, "dp", "tensor"),
        P(None, "dp", "tensor"),
        P("tensor", "dp"),
        P("tensor", "dp"),
        P("dp", "tensor"),
        P("dp", "tensor"),
        P("tensor", "dp"),
        P("tensor", "dp"),
        P(None, "dp"),
        P(None, "dp"),
        P("tensor", None),
        P("tensor", None),
    )
    out_specs = (
        P(("dp", "tensor"), None),
        P(("dp", "tensor"), None),
        P(None, "dp", "tensor"),
        P(None, "dp", "tensor"),
        P(None, "dp", "tensor"),
        P("tensor", "dp"),
        P("tensor", "dp"),
        P("tensor", "dp"),
        P("dp", "tensor"),
        P("dp", "tensor"),
        P("dp", "tensor"),
        P("tensor", "dp"),
        P("tensor", "dp"),
        P("tensor", "dp"),
        P(None, "dp"),
        P(None, "dp"),
        P(None, "dp"),
        P("tensor", None),
        P("tensor", None),
        P("tensor", None),
    )
    return jax.shard_map(
        per_device, mesh=mesh, in_specs=in_specs, out_specs=out_specs, check_vma=False
    )
```

```python
import functools
import math

import jax
import jax.numpy as jnp
import numpy as np
from jax import lax
from jax.experimental import pallas as pl
from jax.experimental.pallas import tpu as pltpu
from jax.sharding import PartitionSpec as P

FF = 2048
WIN = 7
SIDE = 14
SHIFT = 3
STEP = 10


norm_eps = 1e-05
mask_fill = -100.0
beta_one = 0.9
beta_two = 0.999
adam_eps = 1e-08
weight_decay = 0.05
rate_matrix = 0.1
rate_small = 1.0
inv_root_two = 1.0 / math.sqrt(2.0)
inv_root_tau = 1.0 / math.sqrt(2.0 * math.pi)


def axis_bits(size):
    return size.bit_length() - 1


def bit_orders(dp_size, tensor_size):
    dp_bits = [("dp", bit) for bit in reversed(range(axis_bits(dp_size)))]
    tensor_bits = [("tensor", bit) for bit in reversed(range(axis_bits(tensor_size)))]
    if dp_size == 8 and tensor_size == 4:
        z_high, z_low, x_bit = dp_bits
        y_bit, core = tensor_bits
        return (
            (z_high, z_low, x_bit, y_bit, core),
            (z_high, z_low, y_bit, x_bit, core),
            (x_bit, y_bit, z_high, z_low, core),
        )
    core = dp_bits[-1]
    rest = dp_bits[:-1]
    return (
        tuple(rest + tensor_bits + [core]),
        tuple(rest + tensor_bits + [core]),
        tuple(tensor_bits + rest + [core]),
    )


def bit_value(place, bit):
    axis, level = bit
    return (place[axis] // (2**level)) % 2


def slot_of(place, order):
    slot = 0
    for level, bit in enumerate(order):
        slot = slot + bit_value(place, bit) * (2**level)
    return slot


def partner_of(place, bit):
    axis, level = bit
    other = place[axis] + (1 - 2 * bit_value(place, bit)) * (2**level)
    return tuple(other if name == axis else place[name] for name in ("dp", "tensor"))


def greet(place, order):
    barrier = pltpu.get_barrier_semaphore()
    for bit in order:
        pl.semaphore_signal(
            barrier, inc=1, device_id=partner_of(place, bit), device_id_type=pl.DeviceIdType.MESH
        )
    pl.semaphore_wait(barrier, len(order))


def here():
    return {"dp": lax.axis_index("dp"), "tensor": lax.axis_index("tensor")}


def gather_kernel(orders, *refs):
    parts = len(orders)
    ins, outs = refs[:parts], refs[parts : 2 * parts]
    send_sem, recv_sem, own_sem = refs[2 * parts :]
    place = here()
    stages = len(orders[0])
    greet(place, orders[0])
    slots = [slot_of(place, order) for order in orders]
    own_copies = []
    for part in range(parts):
        own = pltpu.make_async_copy(ins[part], outs[part].at[slots[part]], own_sem.at[part])
        own.start()
        own_copies.append(own)
    copies = {}
    for stage in range(stages):
        for part in range(parts):
            if stage == 0:
                source, target = ins[part], outs[part].at[slots[part]]
            else:
                if stage == 1:
                    own_copies[part].wait()
                copies[part, stage - 1].wait_recv()
                first = (slots[part] // (2**stage)) * (2**stage)
                source = target = outs[part].at[pl.ds(first, 2**stage)]
            copy = pltpu.make_async_remote_copy(
                src_ref=source,
                dst_ref=target,
                send_sem=send_sem.at[part, stage],
                recv_sem=recv_sem.at[part, stage],
                device_id=partner_of(place, orders[part][stage]),
                device_id_type=pl.DeviceIdType.MESH,
            )
            copy.start()
            copies[part, stage] = copy
    for part in range(parts):
        copies[part, stages - 1].wait_recv()
    for copy in copies.values():
        copy.wait_send()


def gather_blocks(blocks, orders):
    stages = len(orders[0])
    parts = len(blocks)
    return pl.pallas_call(
        functools.partial(gather_kernel, orders),
        out_shape=[jax.ShapeDtypeStruct((2**stages,) + b.shape, b.dtype) for b in blocks],
        in_specs=[pl.BlockSpec(memory_space=pl.ANY)] * parts,
        out_specs=[pl.BlockSpec(memory_space=pl.ANY)] * parts,
        scratch_shapes=[
            pltpu.SemaphoreType.DMA((parts, stages)),
            pltpu.SemaphoreType.DMA((parts, stages)),
            pltpu.SemaphoreType.DMA((parts,)),
        ],
        compiler_params=pltpu.CompilerParams(collective_id=1, has_side_effects=True),
        name="gather_weights",
    )(*blocks)


def reduce_kernel(orders, *refs):
    parts = len(orders)
    ins, small_in = refs[:parts], refs[parts]
    outs, small_out = refs[parts + 1 : 2 * parts + 1], refs[2 * parts + 1]
    rest = refs[2 * parts + 2 :]
    accs, recvs = rest[:parts], rest[parts : 2 * parts]
    small_acc, small_recv, send_sem, recv_sem = rest[2 * parts :]
    place = here()
    stages = len(orders[0])
    slots = [slot_of(place, order) for order in orders]
    greet(place, orders[0])
    small_acc[0] = small_in[...]
    copies = {}

    def send(part, stage):
        order = orders[part] if part < parts else orders[0]
        bit = order[stages - 1 - stage]
        half = 2 ** (stages - 1 - stage)
        if part == parts:
            source, target = small_acc.at[stage], small_recv.at[stage]
        else:
            mine = bit_value(place, bit)
            source = (ins[part] if stage == 0 else accs[part]).at[pl.ds((1 - mine) * half, half)]
            target = recvs[part].at[pl.ds(half, half)]
        copy = pltpu.make_async_remote_copy(
            src_ref=source,
            dst_ref=target,
            send_sem=send_sem.at[part, stage],
            recv_sem=recv_sem.at[part, stage],
            device_id=partner_of(place, bit),
            device_id_type=pl.DeviceIdType.MESH,
        )
        copy.start()
        copies[part, stage] = copy

    for part in range(parts + 1):
        send(part, 0)
    for stage in range(stages):
        half = 2 ** (stages - 1 - stage)
        for part in range(parts + 1):
            copies[part, stage].wait_recv()
            if part == parts:
                small_acc[stage + 1] = small_acc[stage] + small_recv[stage]
            else:
                mine = bit_value(place, orders[part][stages - 1 - stage])
                source = ins[part] if stage == 0 else accs[part]
                if stage > 0:
                    copies[part, stage].wait_send()

                def add(index, carry):
                    total = source[mine * half + index].astype(jnp.float32) + recvs[part][
                        half + index
                    ].astype(jnp.float32)
                    if stage == stages - 1:
                        outs[part][...] = total
                    else:
                        accs[part][index] = total.astype(jnp.bfloat16)
                    return carry

                lax.fori_loop(0, half, add, 0)
            if stage < stages - 1:
                send(part, stage + 1)
    small_out[...] = small_acc[stages]
    for (part, stage), copy in copies.items():
        if part == parts or stage == 0:
            copy.wait_send()


def reduce_blocks(blocks, small, orders):
    stages = len(orders[0])
    parts = len(blocks)
    count = 2**stages
    vmem = pl.BlockSpec(memory_space=pltpu.VMEM)
    return pl.pallas_call(
        functools.partial(reduce_kernel, orders),
        out_shape=[jax.ShapeDtypeStruct(b.shape[1:], jnp.float32) for b in blocks]
        + [jax.ShapeDtypeStruct(small.shape, jnp.float32)],
        in_specs=[vmem] * (parts + 1),
        out_specs=[vmem] * (parts + 1),
        scratch_shapes=[pltpu.VMEM((count // 2,) + b.shape[1:], jnp.bfloat16) for b in blocks]
        + [pltpu.VMEM(b.shape, jnp.bfloat16) for b in blocks]
        + [
            pltpu.VMEM((stages + 1,) + small.shape, jnp.float32),
            pltpu.VMEM((stages,) + small.shape, jnp.float32),
            pltpu.SemaphoreType.DMA((parts + 1, stages)),
            pltpu.SemaphoreType.DMA((parts + 1, stages)),
        ],
        compiler_params=pltpu.CompilerParams(
            collective_id=2, has_side_effects=True, vmem_limit_bytes=40 * 2**20
        ),
        name="reduce_gradients",
    )(*blocks, small)


def mesh_bits(dp_size, tensor_size):
    return [("dp", bit) for bit in reversed(range(axis_bits(dp_size)))] + [
        ("tensor", bit) for bit in reversed(range(axis_bits(tensor_size)))
    ]


def to_mesh_order(gathered, order, dp_size, tensor_size):
    slot_bits = list(reversed(order))
    wanted = mesh_bits(dp_size, tensor_size)
    count = len(wanted)
    tail = gathered.shape[1:]
    split = gathered.reshape((2,) * count + tail)
    axes = [slot_bits.index(bit) for bit in wanted] + [count + i for i in range(len(tail))]
    return split.transpose(axes).reshape((dp_size, tensor_size) + tail)


def to_slot_order(values, order, dp_size, tensor_size):
    slot_bits = list(reversed(order))
    held = mesh_bits(dp_size, tensor_size)
    count = len(held)
    tail = values.shape[2:]
    split = values.reshape((2,) * count + tail)
    axes = [held.index(bit) for bit in slot_bits] + [count + i for i in range(len(tail))]
    return split.transpose(axes).reshape((2**count,) + tail)


def wide(block):
    rows, columns = block.shape[-2:]
    if rows % 16 == 0:
        return block
    return block.reshape(block.shape[:-2] + (rows * 2, columns // 2))


def region_label(position, image_side, win_side, shift_by):
    return np.where(
        position < image_side - win_side, 0, np.where(position < image_side - shift_by, 1, 2)
    )


def window_tables(win_side, image_side, shift_by):
    cell_total = win_side * win_side
    cell_rows = np.arange(cell_total) // win_side
    cell_cols = np.arange(cell_total) % win_side
    index_table = (cell_rows[:, None] - cell_rows[None, :] + win_side - 1) * (2 * win_side - 1) + (
        cell_cols[:, None] - cell_cols[None, :] + win_side - 1
    )
    per_side = image_side // win_side
    mask_list = []
    for window_row in range(per_side):
        for window_col in range(per_side):
            label_rows = region_label(
                window_row * win_side + cell_rows, image_side, win_side, shift_by
            )
            label_cols = region_label(
                window_col * win_side + cell_cols, image_side, win_side, shift_by
            )
            labels = 3 * label_rows + label_cols
            mask_list.append(np.where(labels[:, None] != labels[None, :], mask_fill, 0.0))
    return (index_table, np.stack(mask_list).astype(np.float32))


def layer_norm(values):
    center = values - jnp.mean(values, axis=-1, keepdims=True)
    spread = lax.rsqrt(jnp.mean(center * center, axis=-1, keepdims=True) + norm_eps)
    return (center * spread, spread)


def norm_back(grad_norm, normed, spread, gain):
    scaled = grad_norm * gain
    return spread * (
        scaled
        - jnp.mean(scaled, axis=-1, keepdims=True)
        - normed * jnp.mean(scaled * normed, axis=-1, keepdims=True)
    )


PAD_ROWS = 208
OUTSIDE = -1e30


def image_tables():
    cells = np.arange(SIDE * SIDE)
    window, cell = cells // (WIN * WIN), cells % (WIN * WIN)
    per_side = SIDE // WIN
    row = (window // per_side * WIN + cell // WIN + SHIFT) % SIDE
    col = (window % per_side * WIN + cell % WIN + SHIFT) % SIDE
    order = np.zeros((PAD_ROWS, SIDE * SIDE), np.float32)
    order[cells, row * SIDE + col] = 1.0
    spread_cells = np.zeros((PAD_ROWS, WIN * WIN), np.float32)
    spread_cells[cells, cell] = 1.0
    mask = np.full((PAD_ROWS, PAD_ROWS), OUTSIDE, np.float32)
    _, mask_table = window_tables(WIN, SIDE, SHIFT)
    size = WIN * WIN
    for index in range(per_side * per_side):
        place = slice(index * size, (index + 1) * size)
        mask[place, place] = mask_table[index]
    return order, spread_cells, mask


def dot_on(left, right, left_dim, right_dim):
    return lax.dot_general(
        left,
        right,
        (((left_dim,), (right_dim,)), ((), ())),
        preferred_element_type=jnp.float32,
    )


def head_probs(queries, key_rows, grid_low, cells, mask, scale):
    bias = dot_on(dot_on(cells, grid_low, 1, 0).astype(jnp.bfloat16), cells, 1, 1)
    scores = dot_on(queries, key_rows, 1, 1) * scale + bias + mask
    terms = jnp.exp(scores - jnp.max(scores, axis=-1, keepdims=True))
    return terms / jnp.sum(terms, axis=-1, keepdims=True)


def attend_kernel(heads, head_size, qkv_ref, grid_ref, cells_ref, mask_ref, out_ref):
    cells, mask = cells_ref[...], mask_ref[...]
    for head in range(heads):
        span = slice(head * head_size, (head + 1) * head_size)
        probs = head_probs(
            qkv_ref[0, :, span], qkv_ref[1, :, span], grid_ref[head], cells, mask, head_size**-0.5
        )
        out_ref[:, span] = dot_on(
            probs.astype(jnp.bfloat16), qkv_ref[2, :, span], 1, 0
        ).astype(jnp.bfloat16)


def attend_back_kernel(
    heads, head_size, qkv_ref, grad_ref, grid_ref, cells_ref, mask_ref, out_ref, grid_out
):
    cells, mask = cells_ref[...], mask_ref[...]
    scale = head_size**-0.5

    @pl.when(pl.program_id(1) == 0)
    def _():
        grid_out[...] = jnp.zeros_like(grid_out)

    for head in range(heads):
        span = slice(head * head_size, (head + 1) * head_size)
        queries, key_rows, val_rows = (qkv_ref[index, :, span] for index in range(3))
        grad = grad_ref[:, span]
        probs = head_probs(queries, key_rows, grid_ref[head], cells, mask, scale)
        grad_probs = dot_on(grad, val_rows, 1, 1)
        inner = jnp.sum(probs * grad_probs, axis=-1, keepdims=True)
        grad_scores = (probs * (grad_probs - inner)).astype(jnp.bfloat16)
        out_ref[0, :, span] = (dot_on(grad_scores, key_rows, 1, 0) * scale).astype(jnp.bfloat16)
        out_ref[1, :, span] = (dot_on(grad_scores, queries, 0, 0) * scale).astype(jnp.bfloat16)
        out_ref[2, :, span] = dot_on(probs.astype(jnp.bfloat16), grad, 0, 0).astype(jnp.bfloat16)
        by_row = dot_on(cells, grad_scores, 0, 0).astype(jnp.bfloat16)
        grid_out[head] += dot_on(by_row, cells, 1, 0)


def attention_call(kernel, qkv, grad, grid_low, cells, mask, head_size):
    heads = 128 // head_size
    rows, channels = qkv.shape[1:]
    size = grid_low.shape[1]
    qkv_spec = pl.BlockSpec((3, PAD_ROWS, 128), lambda group, image: (0, image, group))
    rows_spec = pl.BlockSpec((PAD_ROWS, 128), lambda group, image: (image, group))
    grid_spec = pl.BlockSpec((heads, size, size), lambda group, image: (group, 0, 0))
    fixed = [
        pl.BlockSpec(cells.shape, lambda group, image: (0, 0)),
        pl.BlockSpec(mask.shape, lambda group, image: (0, 0)),
    ]
    if grad is None:
        out_shape = jax.ShapeDtypeStruct((rows, channels), jnp.bfloat16)
        out_specs = rows_spec
        operands, in_specs = (qkv, grid_low, cells, mask), [qkv_spec, grid_spec] + fixed
    else:
        out_shape = [
            jax.ShapeDtypeStruct(qkv.shape, jnp.bfloat16),
            jax.ShapeDtypeStruct(grid_low.shape, jnp.float32),
        ]
        out_specs = [qkv_spec, grid_spec]
        operands = (qkv, grad, grid_low, cells, mask)
        in_specs = [qkv_spec, rows_spec, grid_spec] + fixed
    return pl.pallas_call(
        functools.partial(kernel, heads, head_size),
        grid=(channels // 128, rows // PAD_ROWS),
        out_shape=out_shape,
        in_specs=in_specs,
        out_specs=out_specs,
        compiler_params=pltpu.CompilerParams(vmem_limit_bytes=32 * 2**20),
    )(*operands)


def to_windows(values, order):
    images = values.shape[0] // (SIDE * SIDE)
    split = values.reshape(images, SIDE * SIDE, values.shape[1])
    moved = jnp.einsum("ij,njc->nic", order, split, preferred_element_type=jnp.bfloat16)
    return moved.reshape(images * PAD_ROWS, values.shape[1])


def from_windows(values, order):
    images = values.shape[0] // PAD_ROWS
    split = values.reshape(images, PAD_ROWS, values.shape[1])
    moved = jnp.einsum("ij,nic->njc", order, split, preferred_element_type=jnp.bfloat16)
    return moved.reshape(images * SIDE * SIDE, values.shape[1])


def run_block(
    tokens_in,
    out_grad,
    w_qkv,
    wt_proj,
    w_fc1,
    wt_fc2,
    small_all,
    table_low,
):
    row_count = tokens_in.shape[0]
    channels = tokens_in.shape[1]
    heads = table_low.shape[0]
    head_size = channels // heads
    small_vals = small_all.astype(jnp.float32)
    gain_one = small_vals[0]
    bias_one = small_vals[1]
    gain_two = small_vals[2]
    bias_two = small_vals[3]
    bias_query = small_vals[4]
    bias_value = small_vals[5]
    bias_proj = small_vals[6]
    bias_out = small_vals[7]
    bias_hidden = small_vals[8:].reshape(-1)
    index_table, _ = window_tables(WIN, SIDE, SHIFT)
    table_size = (2 * WIN - 1) ** 2
    cell_count = WIN * WIN
    lookup_np = index_table.reshape(-1)[:, None] == np.arange(table_size)[None, :]
    lookup = jnp.asarray(lookup_np.astype(np.float32))
    order_np, cells_np, mask_np = image_tables()
    order = jnp.asarray(order_np, jnp.bfloat16)
    cells = jnp.asarray(cells_np, jnp.bfloat16)
    mask = jnp.asarray(mask_np)
    grid_low = lax.dot_general(
        table_low,
        lookup.astype(jnp.bfloat16),
        (((1,), (1,)), ((), ())),
        preferred_element_type=jnp.float32,
    )
    grid_low = grid_low.astype(jnp.bfloat16).reshape(heads, cell_count, cell_count)
    normed_one, spread_one = layer_norm(tokens_in)
    act_low = (normed_one * gain_one + bias_one).astype(jnp.bfloat16)
    act_win = to_windows(act_low, order)
    bias_qkv = jnp.stack([bias_query, jnp.zeros_like(bias_query), bias_value])[:, None]
    qkv = jnp.einsum("rc,kcd->krd", act_win, w_qkv, preferred_element_type=jnp.float32)
    qkv = (qkv + bias_qkv).astype(jnp.bfloat16)
    attn_win = attention_call(attend_kernel, qkv, None, grid_low, cells, mask, head_size)
    attn_tok = from_windows(attn_win, order)
    proj_sum = lax.dot_general(
        attn_tok, wt_proj, (((1,), (1,)), ((), ())), preferred_element_type=jnp.float32
    )
    middle = tokens_in + proj_sum + bias_proj
    normed_two, spread_two = layer_norm(middle)
    mixed = (normed_two * gain_two + bias_two).astype(jnp.bfloat16)
    mixed_all = mixed
    hidden = jnp.dot(mixed_all, w_fc1, preferred_element_type=jnp.float32) + bias_hidden
    gelu_out = jax.nn.gelu(hidden, approximate=False).astype(jnp.bfloat16)
    mlp_sum = lax.dot_general(
        gelu_out, wt_fc2, (((1,), (1,)), ((), ())), preferred_element_type=jnp.float32
    )
    result = middle + mlp_sum + bias_out
    grad_low = out_grad.astype(jnp.bfloat16)
    grad_all = grad_low
    grad_w2 = lax.dot_general(
        grad_all, gelu_out, (((0,), (0,)), ((), ())), preferred_element_type=jnp.float32
    )
    grad_gelu = lax.dot_general(
        grad_all, wt_fc2, (((1,), (0,)), ((), ())), preferred_element_type=jnp.float32
    )
    slope = (
        0.5 * (1.0 + lax.erf(hidden * inv_root_two))
        + hidden * jnp.exp(-0.5 * hidden * hidden) * inv_root_tau
    )
    grad_hidden = (grad_gelu * slope).astype(jnp.bfloat16)
    grad_w1 = lax.dot_general(
        mixed_all, grad_hidden, (((0,), (0,)), ((), ())), preferred_element_type=jnp.float32
    )
    grad_bias_hidden = jnp.sum(grad_hidden.astype(jnp.float32), axis=0)
    grad_mixed = lax.dot_general(
        grad_hidden, w_fc1, (((1,), (1,)), ((), ())), preferred_element_type=jnp.float32
    )
    grad_gain_two = jnp.sum(grad_mixed * normed_two, axis=0)
    grad_bias_two = jnp.sum(grad_mixed, axis=0)
    grad_middle = out_grad + norm_back(grad_mixed, normed_two, spread_two, gain_two)
    grad_branch = grad_middle.astype(jnp.bfloat16)
    grad_branch_all = grad_branch
    grad_wp = lax.dot_general(
        grad_branch_all, attn_tok, (((0,), (0,)), ((), ())), preferred_element_type=jnp.float32
    )
    grad_attn = lax.dot_general(
        grad_branch_all, wt_proj, (((1,), (0,)), ((), ())), preferred_element_type=jnp.float32
    ).astype(jnp.bfloat16)
    grad_qkv, grad_grid = attention_call(
        attend_back_kernel, qkv, to_windows(grad_attn, order), grid_low, cells, mask, head_size
    )
    grad_wqkv = jnp.einsum("rc,krd->kcd", act_win, grad_qkv, preferred_element_type=jnp.float32)
    grad_bias_query = jnp.sum(grad_qkv[0].astype(jnp.float32), axis=0)
    grad_bias_value = jnp.sum(grad_qkv[2].astype(jnp.float32), axis=0)
    grad_act = sum(
        dot_on(from_windows(grad_qkv[index], order), w_qkv[index], 1, 1) for index in range(3)
    )
    grad_gain_one = jnp.sum(grad_act * normed_one, axis=0)
    grad_bias_one = jnp.sum(grad_act, axis=0)
    grad_tokens = grad_middle + norm_back(grad_act, normed_one, spread_one, gain_one)
    grad_bias_proj = jnp.sum(grad_branch.astype(jnp.float32), axis=0)
    grad_bias_out = jnp.sum(grad_low.astype(jnp.float32), axis=0)
    grad_table = lax.dot_general(
        grad_grid.reshape(heads, cell_count * cell_count),
        lookup,
        (((1,), (0,)), ((), ())),
        precision=lax.Precision.HIGHEST,
    )
    leading_rows = jnp.stack(
        [
            grad_gain_one,
            grad_bias_one,
            grad_gain_two,
            grad_bias_two,
            grad_bias_query,
            grad_bias_value,
            grad_bias_proj,
            grad_bias_out,
        ]
    )
    small_grad = jnp.concatenate(
        [leading_rows, grad_bias_hidden.reshape(FF // channels, channels)], axis=0
    )
    return (result, grad_tokens, (grad_wqkv, grad_wp, grad_w1, grad_w2, small_grad, grad_table))


def adam_update(weight, grad, first, second, rate):
    first_new = beta_one * first + (1.0 - beta_one) * grad
    second_new = beta_two * second + (1.0 - beta_two) * grad * grad
    first_hat = first_new / (1.0 - beta_one**STEP)
    second_hat = second_new / (1.0 - beta_two**STEP)
    weight_new = weight - rate * (
        first_hat / (jnp.sqrt(second_hat) + adam_eps) + weight_decay * weight
    )
    return (first_new, second_new, weight_new)


def per_device(
    tokens_in,
    out_grad,
    w_qkv,
    w_proj,
    w_fc1,
    w_fc2,
    small_params,
    bias_table,
    qkv_first,
    qkv_second,
    proj_first,
    proj_second,
    fc1_first,
    fc1_second,
    fc2_first,
    fc2_second,
    small_first,
    small_second,
    table_first,
    table_second,
):
    dp_size, tensor_size = lax.axis_size("dp"), lax.axis_size("tensor")
    orders = bit_orders(dp_size, tensor_size)
    rows, head_cols = w_qkv.shape[1:]
    hidden_cols = w_fc1.shape[1]
    channels = tokens_in.shape[1]
    small_rows = small_params.shape[0]
    heads_here, table_size = bias_table.shape
    block_attn = jnp.concatenate([w_qkv, w_proj.T[None]], axis=0).astype(jnp.bfloat16)
    block_attn = block_attn.reshape(4 * rows, head_cols)
    block_one = wide(w_fc1.astype(jnp.bfloat16))
    block_two = wide(w_fc2.T.astype(jnp.bfloat16))
    table_wide = jnp.pad(bias_table, ((0, 0), (0, 256 - table_size))).reshape(-1, 128)
    block_small = jnp.concatenate(
        [
            jnp.pad(small_params, ((0, 16 - small_rows), (0, 128 - rows))),
            jnp.pad(table_wide, ((0, 16 - table_wide.shape[0]), (0, 0))),
        ],
        axis=0,
    ).astype(jnp.bfloat16)
    gathered = gather_blocks(
        (block_attn, block_one, block_two, block_small), orders + (orders[0],)
    )
    all_attn, all_one, all_two, all_small = (
        to_mesh_order(values, order, dp_size, tensor_size)
        for values, order in zip(gathered, orders + (orders[0],))
    )
    all_attn = all_attn.reshape(dp_size, tensor_size, 4, rows, head_cols)
    all_attn = all_attn.transpose(2, 0, 3, 1, 4).reshape(4, channels, channels)
    all_one, all_two = (
        values.reshape(dp_size, tensor_size, rows, hidden_cols)
        .transpose(0, 2, 1, 3)
        .reshape(channels, FF)
        for values in (all_one, all_two)
    )
    small_all = all_small[:, 0, :small_rows, :rows].transpose(1, 0, 2)
    small_all = small_all.reshape(small_rows, channels)
    table_low = all_small[0, :, 16 : 16 + table_wide.shape[0]]
    table_low = table_low.reshape(tensor_size * heads_here, 256)[:, :table_size]
    result, grad_tokens, grads = run_block(
        tokens_in,
        out_grad,
        all_attn[:3],
        all_attn[3],
        all_one,
        all_two,
        small_all,
        table_low,
    )
    grad_wqkv, grad_wp, grad_w1, grad_w2, small_grad, grad_table = grads
    pack_attn = jnp.concatenate([grad_wqkv, grad_wp[None]], axis=0).astype(jnp.bfloat16)
    pack_attn = pack_attn.reshape(4, dp_size, rows, tensor_size, head_cols)
    pack_attn = pack_attn.transpose(1, 3, 0, 2, 4)
    pack_attn = pack_attn.reshape(dp_size, tensor_size, 4 * rows, head_cols)
    pack_one, pack_two = (
        wide(
            values.astype(jnp.bfloat16)
            .reshape(dp_size, rows, tensor_size, hidden_cols)
            .transpose(0, 2, 1, 3)
        )
        for values in (grad_w1, grad_w2)
    )
    packs = tuple(
        to_slot_order(values, order, dp_size, tensor_size)
        for values, order in zip((pack_attn, pack_one, pack_two), orders)
    )
    small_flat = small_grad.reshape(-1, 128)
    pack_small = jnp.concatenate(
        [small_flat, jnp.pad(grad_table, ((0, 0), (0, 256 - table_size))).reshape(-1, 128)], axis=0
    )
    sum_attn, sum_one, sum_two, sum_small = reduce_blocks(packs, pack_small, orders)
    sum_attn = sum_attn.reshape(4, rows, head_cols)
    shard_qkv, shard_proj = sum_attn[:3], sum_attn[3].T
    shard_one = sum_one.reshape(rows, hidden_cols)
    shard_two = sum_two.reshape(rows, hidden_cols).T
    small_total = sum_small[: small_flat.shape[0]].reshape(small_rows, channels)
    shard_small = lax.dynamic_slice_in_dim(small_total, lax.axis_index("dp") * rows, rows, 1)
    table_total = sum_small[small_flat.shape[0] :].reshape(-1, 256)[:, :table_size]
    table_grad = lax.dynamic_slice_in_dim(
        table_total, lax.axis_index("tensor") * heads_here, heads_here, 0
    )
    qkv_first_new, qkv_second_new, qkv_new = adam_update(
        w_qkv, shard_qkv, qkv_first, qkv_second, rate_matrix
    )
    proj_first_new, proj_second_new, proj_new = adam_update(
        w_proj, shard_proj, proj_first, proj_second, rate_matrix
    )
    fc1_first_new, fc1_second_new, fc1_new = adam_update(
        w_fc1, shard_one, fc1_first, fc1_second, rate_matrix
    )
    fc2_first_new, fc2_second_new, fc2_new = adam_update(
        w_fc2, shard_two, fc2_first, fc2_second, rate_matrix
    )
    small_first_new, small_second_new, small_new = adam_update(
        small_params, shard_small, small_first, small_second, rate_small
    )
    table_first_new, table_second_new, table_new = adam_update(
        bias_table, table_grad, table_first, table_second, rate_small
    )
    return (
        result,
        grad_tokens,
        qkv_first_new,
        qkv_second_new,
        qkv_new,
        proj_first_new,
        proj_second_new,
        proj_new,
        fc1_first_new,
        fc1_second_new,
        fc1_new,
        fc2_first_new,
        fc2_second_new,
        fc2_new,
        small_first_new,
        small_second_new,
        small_new,
        table_first_new,
        table_second_new,
        table_new,
    )


def solution(mesh):
    in_specs = (
        P(("dp", "tensor"), None),
        P(("dp", "tensor"), None),
        P(None, "dp", "tensor"),
        P("tensor", "dp"),
        P("dp", "tensor"),
        P("tensor", "dp"),
        P(None, "dp"),
        P("tensor", None),
        P(None, "dp", "tensor"),
        P(None, "dp", "tensor"),
        P("tensor", "dp"),
        P("tensor", "dp"),
        P("dp", "tensor"),
        P("dp", "tensor"),
        P("tensor", "dp"),
        P("tensor", "dp"),
        P(None, "dp"),
        P(None, "dp"),
        P("tensor", None),
        P("tensor", None),
    )
    out_specs = (
        P(("dp", "tensor"), None),
        P(("dp", "tensor"), None),
        P(None, "dp", "tensor"),
        P(None, "dp", "tensor"),
        P(None, "dp", "tensor"),
        P("tensor", "dp"),
        P("tensor", "dp"),
        P("tensor", "dp"),
        P("dp", "tensor"),
        P("dp", "tensor"),
        P("dp", "tensor"),
        P("tensor", "dp"),
        P("tensor", "dp"),
        P("tensor", "dp"),
        P(None, "dp"),
        P(None, "dp"),
        P(None, "dp"),
        P("tensor", None),
        P("tensor", None),
        P("tensor", None),
    )
    return jax.shard_map(
        per_device, mesh=mesh, in_specs=in_specs, out_specs=out_specs, check_vma=False
    )
```
